128 devices in a mesh: ctx: 32 (over x, y, core), tp: 4 (over z).
Axes of the slice: x: 4, y: 4, z: 4, core: 2. Of those that a mesh axis runs over, the one named last changes fastest.
Arguments:
- context: bfloat16 [12288, 8192], P('ctx', 'tp'), may hold values from -170 to 170
- visual: bfloat16 [4096, 8192], P('ctx', 'tp'), may hold values from -170 to 170
- visual_slots: int32 [4096], P('ctx'), may hold values from 0 to 12287, as said below
- norm_gain: bfloat16 [8192], replicated, may hold values from 0.099609375 to 1.8984375
- key_value_weight: bfloat16 [8192, 2048], P(None, 'tp'), may hold values from -0.0625 to 0.0625
- key_value_bias: bfloat16 [2048], P('tp'), may hold values from -4 to 4
- queries: bfloat16 [4096, 8192], P('ctx', 'tp'), may hold values from -110 to 110
- key_segments: int32 [12288], P('ctx'), may hold values from 0 to 15, never falling along the last dimension, each value on 1 to 1536 neighbouring positions
- query_segments: int32 [4096], P('ctx'), may hold values from 0 to 15, never falling along the last dimension, each value on 1 to 512 neighbouring positions
Outputs:
- attention_out: bfloat16 [4096, 8192], P('ctx', 'tp')
The draws below stay inside these ranges and needn't reach their ends.
Inputs may be any that keep to these rules, and one draw needn't show every extreme that they name: `visual_slots`: all entries are distinct. The 128 entries held by each index of ctx name exactly 4 rows held by each index of ctx. `key_segments`: never falling along the context, starting at 0. `query_segments`: never falling along the query tokens.
All inputs are finite; a program needn't handle non-finite values.
Results may differ from the reference program's by a relative error of at most 0.012.
Values may be sent and summed in bfloat16 or wider, within the bound.
No kernel may reach another device: no remote copies, remote signals or barrier semaphores. Data moves between devices by JAX's collectives and lax.ppermute only.
A program may use at most 128 MiB of HBM per device.

```python
import math
import jax
import jax.numpy as jnp
import numpy as np
from jax import lax

D = 8192
HEADS = 64
KV_HEADS = 8
HEAD = 128
SEGS = 16
CTX_DEV = 384
VIS_DEV = 128
CONTEXT = 12288
QUERIES = 4096
VISUAL = 4096
N_CTX = 32


def clipped_normal(key, rows, cols):
    return jnp.clip(jax.random.normal(key, (rows, cols), jnp.float32), -6.0, 6.0)


def draw_context(key, part):
    key = jax.random.fold_in(key, 1)
    return clipped_normal(key, CONTEXT, D).astype(jnp.bfloat16)


def draw_visual(key, part):
    key = jax.random.fold_in(key, 2)
    return clipped_normal(key, VISUAL, D).astype(jnp.bfloat16)


def draw_queries(key, part):
    key = jax.random.fold_in(key, 3)
    return clipped_normal(key, QUERIES, HEADS * HEAD).astype(jnp.bfloat16)


def draw_visual_slots(key, part):
    key = jax.random.fold_in(key, 4)
    source_key, dest_key = jax.random.split(key)
    per_peer = VIS_DEV // N_CTX
    send_order = jax.vmap(lambda sub_key: jax.random.permutation(sub_key, VIS_DEV))(jax.random.split(source_key, N_CTX))
    offsets = jax.vmap(lambda sub_key: jax.random.permutation(sub_key, CTX_DEV)[:VIS_DEV])(jax.random.split(dest_key, N_CTX))
    owners = send_order // per_peer
    arrival = jnp.arange(N_CTX, dtype=jnp.int32)[:, None] * per_peer + send_order % per_peer
    slots_all = owners * CTX_DEV + offsets[owners, arrival]
    return slots_all.reshape(-1).astype(jnp.int32)


def steps_of(stream_key, extent, cuts, least, top_value):
    def one(position, shards_of):
        heights = jax.random.uniform(jax.random.fold_in(jax.random.fold_in(stream_key, 6), position), (shards_of,), jnp.float32, least / len(cuts), top_value / len(cuts))
        return jnp.repeat(jnp.exp(heights), extent[position] // shards_of).reshape((-1,) + (1,) * (len(extent) - position - 1))

    gain = one(*cuts[0])
    for cut in cuts[1:]:
        gain = gain * one(*cut)
    return gain


def length_profile(amount, total, reach, skew):
    portions = [(1 << 20) // math.isqrt(grade ** skew) + 1 for grade in range(2, amount + 1)]
    surplus, counts = total - reach - (amount - 1), [1] * (amount - 1)
    while surplus > 0:
        movable = [i for i in range(amount - 1) if counts[i] < reach]
        whole, budget = sum([portions[i] for i in movable]), surplus
        for i in movable:
            addition = min(reach - counts[i], max(1, budget * portions[i] // whole), surplus)
            counts[i] = counts[i] + addition
            surplus = surplus - addition
    return np.array([reach] + counts)


def uneven(rng, amount, total, limit, lean):
    if amount == 2:
        one = jax.random.randint(rng, (), max(1, total - limit), min(limit, total - 1) + 1)
        return jnp.stack([one, total - one])
    tallies = jnp.asarray(length_profile(amount, total, limit, lean), jnp.int32)
    twos = (amount - 1) // 2
    source_of, taker = tallies[1:1 + 2 * twos:2], tallies[2:2 + 2 * twos:2]
    room = jnp.minimum(source_of - 1, limit - taker)
    moved = jax.random.randint(jax.random.fold_in(rng, 1), (twos,), 0, 1 << 20) % (room + 1)
    tallies = tallies.at[1:1 + 2 * twos:2].set(source_of - moved).at[2:2 + 2 * twos:2].set(taker + moved)
    return tallies[jax.random.permutation(jax.random.fold_in(rng, 2), amount)]


def gaussian(rng, dims, scale, most, pieces=(), kind=jnp.bfloat16):
    loudness = steps_of(rng, dims, pieces, -0.22, 0.18) if pieces else 1.0
    entries = jax.random.normal(rng, dims, jnp.float32) * scale * loudness
    return jnp.minimum(jnp.maximum(entries, -most), most).astype(kind)


def setup_inputs(seed: int = 0) -> dict:
    key_list = jax.random.split(jax.random.key(seed), 10)
    return {
        "context": draw_context(jax.random.fold_in(key_list[9], 71), 0),
        "visual": draw_visual(jax.random.fold_in(key_list[9], 71), 0),
        "visual_slots": draw_visual_slots(jax.random.fold_in(key_list[9], 71), 0),
        "norm_gain": jnp.clip(1.0 + 0.18 * jax.random.normal(key_list[3], (D,), jnp.float32), 0.099609375, 1.8984375).astype(jnp.bfloat16),
        "key_value_weight": gaussian(key_list[4], (D, 2 * KV_HEADS * HEAD), D ** -0.5, 0.0625, ((1, 4),)),
        "key_value_bias": gaussian(key_list[5], (2 * KV_HEADS * HEAD,), 1.0, 4.0, ((0, 4),)),
        "queries": draw_queries(jax.random.fold_in(key_list[9], 71), 0),
        "key_segments": jnp.searchsorted(jnp.cumsum(uneven(key_list[7], SEGS, CONTEXT, 2 * CONTEXT // SEGS, 2)), jnp.arange(CONTEXT), side="right").astype(jnp.int32),
        "query_segments": jnp.searchsorted(jnp.cumsum(uneven(key_list[8], SEGS, QUERIES, 2 * QUERIES // SEGS, 2)), jnp.arange(QUERIES), side="right").astype(jnp.int32),
    }


def rotate(values, positions):
    half_dim = values.shape[-1] // 2
    inv_freq = jnp.exp(jnp.arange(half_dim).astype(jnp.float32) * (-2.0 * math.log(1000000.0) / values.shape[-1]))
    angles = positions[:, None] * inv_freq[None, :]
    cosine = jnp.cos(angles)[:, None, :]
    sine_val = jnp.sin(angles)[:, None, :]
    lower_half = values[..., :half_dim]
    upper_half = values[..., half_dim:]
    return jnp.concatenate([lower_half * cosine - upper_half * sine_val, upper_half * cosine + lower_half * sine_val], axis=-1)

def project_keys(merged, norm_gain, key_value_weight, key_value_bias, positions):
    widened = merged.astype(jnp.float32)
    normed = (widened * lax.rsqrt(lax.optimization_barrier(jnp.mean(widened * widened, axis=-1, keepdims=True)) + 1e-06) * norm_gain.astype(jnp.float32)).astype(jnp.bfloat16)
    projected = jnp.dot(normed, key_value_weight, preferred_element_type=jnp.float32) + key_value_bias.astype(jnp.float32)
    projected = projected.reshape(merged.shape[0], -1, 2, HEAD)
    rotated = rotate(projected[:, :, 0], positions)
    return jnp.stack([rotated, projected[:, :, 1]], axis=2).astype(jnp.bfloat16)

def reference(context, visual, visual_slots, norm_gain, key_value_weight, key_value_bias, queries, key_segments, query_segments):
    merged = context.at[visual_slots].set(visual)
    positions = jnp.arange(CONTEXT).astype(jnp.float32)
    key_value = project_keys(merged, norm_gain, key_value_weight, key_value_bias, positions)
    key_heads = jnp.transpose(key_value[:, :, 0], (1, 0, 2))
    value_heads = jnp.transpose(key_value[:, :, 1], (1, 0, 2))
    query_heads = jnp.transpose(queries.reshape(QUERIES, HEADS, HEAD), (1, 0, 2))
    group_of = (jnp.arange(HEADS) // (HEADS // KV_HEADS)).astype(jnp.int32)
    visible = key_segments[None, :] <= query_segments[:, None]

    def one_head(operands):
        query_head, group_idx = operands
        key_head = key_heads[group_idx]
        value_head = value_heads[group_idx]
        scores = jnp.dot(query_head, key_head.T, preferred_element_type=jnp.float32) * HEAD ** (-0.5)
        row_max = lax.optimization_barrier(jnp.max(jnp.where(visible, scores, -jnp.inf), axis=-1, keepdims=True))
        weights = jnp.where(visible, jnp.exp(scores - row_max), 0.0)
        totals = lax.optimization_barrier(jnp.sum(weights, axis=-1, keepdims=True))
        attended = jnp.dot(weights.astype(jnp.bfloat16), value_head, preferred_element_type=jnp.float32)
        return attended / totals
    outputs = lax.map(one_head, (query_heads, group_of))
    return jnp.transpose(outputs, (1, 0, 2)).reshape(QUERIES, HEADS * HEAD).astype(jnp.bfloat16)
```

```python
import functools
import math

import jax
import jax.numpy as jnp
from jax import lax
from jax.experimental import pallas as pl
from jax.experimental.pallas import tpu as pltpu
from jax.sharding import PartitionSpec as P

HEAD = 128
BF = jnp.bfloat16
F32 = jnp.float32
NEG = -1e30
KEY_SCALE = HEAD**-0.5 * math.log2(math.e)
ROWS = 128
PACK = 144
SHIFTS = (0, 1, -1, 2)
VMEM = 48 * 1024 * 1024


def index_of(x, y, core):
    return ((x % 4) * 4 + y % 4) * 2 + core


def devices_of_ctx():
    return [(x, y, core) for x in range(4) for y in range(4) for core in range(2)]


def swap_cores(value):
    perm = [(index_of(x, y, c), index_of(x, y, 1 - c)) for x, y, c in devices_of_ctx()]
    return lax.ppermute(value, "ctx", perm)


def shift_xy(value, by_x, by_y):
    perm = [
        (index_of(x, y, c), index_of(x + by_x, y + by_y, c)) for x, y, c in devices_of_ctx()
    ]
    return lax.ppermute(value, "ctx", perm)


def shift_keys(value, by):
    perm = [
        (index_of(x, y, c), index_of(x + by, y, c) if c == 0 else index_of(x, y + by, c))
        for x, y, c in devices_of_ctx()
    ]
    return lax.ppermute(value, "ctx", perm)


def shift_queries(value, by):
    perm = [
        (index_of(x, y, c), index_of(x, y + by, c) if c == 0 else index_of(x + by, y, c))
        for x, y, c in devices_of_ctx()
    ]
    return lax.ppermute(value, "ctx", perm)


def shift_z(value, by):
    return lax.ppermute(value, "tp", [(i, (i + by) % 4) for i in range(4)])


def gather_features(rows):
    half = rows.shape[0] // 2
    low = shift_z(rows, 1)
    high = shift_z(rows, -1)
    far_low = shift_z(low[:half], 1)
    far_high = shift_z(high[half:], -1)
    return rows, low, high, far_low, far_high


def gather_meta(meta):
    line = jnp.stack([meta] + [shift_xy(meta, k, 0) for k in (1, -1, 2)])
    plane = jnp.stack([line] + [shift_xy(line, 0, k) for k in (1, -1, 2)])
    return jnp.stack([plane, swap_cores(plane)])


def compact_kernel(first_ref, slots_ref, context_ref, rows_ref, positions_ref):
    total, kept = context_ref.shape[0], rows_ref.shape[0]
    place = lax.broadcasted_iota(jnp.int32, (total, HEAD), 0) + first_ref[0]
    hit = jnp.zeros((total, HEAD), F32)
    for i in range(slots_ref.shape[0]):
        hit = jnp.where(place == slots_ref[i : i + 1, :], 1.0, hit)
    hit = jnp.max(hit, axis=1, keepdims=True)
    keep = jnp.broadcast_to(1.0 - hit, (total, HEAD)).astype(BF)
    row = lax.broadcasted_iota(jnp.int32, (total, total), 0)
    col = lax.broadcasted_iota(jnp.int32, (total, total), 1)
    over_rows = (((0,), (0,)), ((), ()))
    before = lax.dot_general(
        keep, (row < col).astype(F32).astype(BF), over_rows, preferred_element_type=F32
    )
    itself = lax.dot_general(
        keep, (row == col).astype(F32).astype(BF), over_rows, preferred_element_type=F32
    )
    rank = jnp.where(itself > 0.5, before, -1.0)[0:1, :]
    want = lax.broadcasted_iota(jnp.int32, (kept, total), 0).astype(F32)
    pick = jnp.where(rank == want, 1.0, 0.0)
    source = lax.broadcasted_iota(jnp.int32, (kept, total), 1).astype(F32)
    positions_ref[...] = jnp.broadcast_to(
        jnp.sum(pick * source, axis=1, keepdims=True), (kept, HEAD)
    ) + first_ref[0].astype(F32)
    rows_ref[...] = jnp.dot(pick.astype(BF), context_ref[...], preferred_element_type=F32).astype(
        BF
    )


def compact(context, slots, first_row, kept):
    return pl.pallas_call(
        compact_kernel,
        out_shape=(
            jax.ShapeDtypeStruct((kept, context.shape[1]), BF),
            jax.ShapeDtypeStruct((kept, HEAD), F32),
        ),
        in_specs=[
            pl.BlockSpec(memory_space=pltpu.SMEM),
            pl.BlockSpec(memory_space=pltpu.VMEM),
            pl.BlockSpec(memory_space=pltpu.VMEM),
        ],
        out_specs=[pl.BlockSpec(memory_space=pltpu.VMEM)] * 2,
        compiler_params=pltpu.CompilerParams(vmem_limit_bytes=VMEM),
        name="compact",
    )(first_row.reshape(1), slots, context)


def project_kernel(
    where_ref,
    own_ref,
    low_ref,
    high_ref,
    far_low_ref,
    far_high_ref,
    gain_ref,
    weight_ref,
    bias_ref,
    cosine_ref,
    sine_ref,
    segment_ref,
    mine_ref,
    other_ref,
    scale_ref,
    total_ref,
):
    step = pl.program_id(0)
    features = own_ref.shape[1]
    half = ROWS // 2

    @pl.when(step == 0)
    def _():
        def squares(ref):
            wide = ref[...].astype(F32)
            return jnp.sum(wide * wide, axis=1, keepdims=True)

        far = jnp.concatenate([squares(far_low_ref), squares(far_high_ref)], axis=0)
        mean = (squares(own_ref) + squares(low_ref) + squares(high_ref) + far) / (4 * features)
        scale_ref[...] = jnp.broadcast_to(lax.rsqrt(mean + 1e-06), (ROWS, HEAD))
        total_ref[...] = jnp.zeros_like(total_ref)

    gain = gain_ref[0].astype(F32)

    def add(ref, start, count):
        normed = (
            ref[...].astype(F32) * scale_ref[pl.ds(start, count), 0:1] * gain
        ).astype(BF)
        total_ref[pl.ds(start, count), :] += jnp.dot(
            normed, weight_ref[...], preferred_element_type=F32
        )

    @pl.when(step == 0)
    def _():
        add(own_ref, 0, ROWS)

    @pl.when(step == 1)
    def _():
        add(low_ref, 0, ROWS)

    @pl.when(step == 2)
    def _():
        add(high_ref, 0, ROWS)

    @pl.when(step == 3)
    def _():
        add(far_low_ref, 0, half)
        add(far_high_ref, half, half)
        cosine, sine = cosine_ref[...], sine_ref[...]
        packed = []
        for head in range(2):
            left = head * 2 * HEAD
            key = total_ref[:, left : left + HEAD] + bias_ref[:, left : left + HEAD].astype(F32)
            value = total_ref[:, left + HEAD : left + 2 * HEAD] + bias_ref[
                :, left + HEAD : left + 2 * HEAD
            ].astype(F32)
            key = key * cosine + pltpu.roll(key, HEAD // 2, 1) * sine
            packed.append(jnp.concatenate([key, value], axis=1).astype(BF))
        mine = where_ref[0] == 0
        mine_ref[0:ROWS, :] = jnp.where(mine, packed[0], packed[1])
        other_ref[0:ROWS, :] = jnp.where(mine, packed[1], packed[0])
        mine_ref[ROWS:PACK, :] = segment_ref[...]
        other_ref[ROWS:PACK, :] = segment_ref[...]


def project(where, parts, gain, weight, bias, cosine, sine, segment):
    features, columns = parts[0].shape[1], weight.shape[1]

    def slice_of(step, where_ref):
        away = jnp.where(step == 1, 3, jnp.where(step == 2, 1, jnp.where(step == 3, 2, 0)))
        return lax.rem(where_ref[1] + away, 4)

    whole = lambda step, where_ref: (0, 0)
    spec = pltpu.PrefetchScalarGridSpec(
        num_scalar_prefetch=1,
        grid=(4,),
        in_specs=[pl.BlockSpec(part.shape, whole) for part in parts]
        + [
            pl.BlockSpec((1, 1, features), lambda s, w: (slice_of(s, w), 0, 0)),
            pl.BlockSpec((features, columns), lambda s, w: (slice_of(s, w), 0)),
            pl.BlockSpec((1, columns), whole),
            pl.BlockSpec((ROWS, HEAD), whole),
            pl.BlockSpec((ROWS, HEAD), whole),
            pl.BlockSpec((PACK - ROWS, 2 * HEAD), whole),
        ],
        out_specs=[pl.BlockSpec((PACK, 2 * HEAD), whole)] * 2,
        scratch_shapes=[pltpu.VMEM((ROWS, HEAD), F32), pltpu.VMEM((ROWS, columns), F32)],
    )
    return pl.pallas_call(
        project_kernel,
        grid_spec=spec,
        out_shape=(jax.ShapeDtypeStruct((PACK, 2 * HEAD), BF),) * 2,
        compiler_params=pltpu.CompilerParams(vmem_limit_bytes=VMEM),
        cost_estimate=pl.CostEstimate(
            flops=2 * ROWS * 4 * features * columns,
            bytes_accessed=2 * 4 * features * (columns + ROWS),
            transcendentals=0,
        ),
        name="project",
    )(
        where,
        *parts,
        gain.reshape(4, 1, features),
        weight,
        bias.reshape(1, columns),
        cosine,
        sine,
        segment,
    )


def attend_kernel(first, last, blocks, *refs):
    query_segments_ref, query_ref = refs[:2]
    key_refs = refs[2 : 2 + blocks]
    refs = refs[2 + blocks :]
    if not first:
        sum_in_ref, stat_in_ref = refs[:2]
        refs = refs[2:]
    if last:
        out_ref = refs[0]
        refs = refs[1:]
    else:
        sum_out_ref, stat_out_ref = refs[:2]
        refs = refs[2:]
    key_ref, value_ref, segment_ref, bias_ref = refs
    keys = key_ref.shape[0]

    @pl.when(pl.program_id(0) == 0)
    def _():
        for i, ref in enumerate(key_refs):
            for j in range(2):
                start = (2 * i + j) * ROWS
                key_ref[start : start + ROWS, :] = ref[j, 0:ROWS, 0:HEAD]
                value_ref[start : start + ROWS, 0:HEAD] = ref[j, 0:ROWS, HEAD:]
                segment_ref[:, start : start + ROWS] = jnp.broadcast_to(
                    ref[j, ROWS:PACK, 0:ROWS].astype(F32)[0:1, :], (8, ROWS)
                )
        value_ref[:, HEAD:] = jnp.ones((keys, HEAD), BF)

    count = query_ref.shape[1]
    query_segments = query_segments_ref[0]
    bias_ref[...] = jnp.where(segment_ref[0:1, :] <= query_segments[:, 0:1], 0.0, NEG)
    lane = lax.broadcasted_iota(jnp.int32, (count, HEAD), 1)
    stat = jnp.zeros((count, HEAD), F32)
    for head in range(query_ref.shape[2] // HEAD):
        left = head * HEAD
        scores = lax.dot_general(
            query_ref[0, :, left : left + HEAD],
            key_ref[...],
            (((1,), (1,)), ((), ())),
            preferred_element_type=F32,
        )
        scores = scores + bias_ref[...]
        row_max = jnp.max(scores, axis=1, keepdims=True)
        if not first:
            before = stat_in_ref[0, :, head : head + 1]
            row_max = jnp.maximum(row_max, before)
        weights = jnp.exp2(scores - row_max).astype(BF)
        summed = jnp.dot(weights, value_ref[...], preferred_element_type=F32)
        total, summed = summed[:, HEAD : HEAD + 1], summed[:, 0:HEAD]
        if not first:
            factor = jnp.exp2(before - row_max)
            total = total + factor * stat_in_ref[0, :, 8 + head : 9 + head]
            summed = summed + factor * sum_in_ref[0, :, left : left + HEAD]
        if last:
            out_ref[0, :, left : left + HEAD] = (summed / total).astype(BF)
            level = row_max + jnp.log2(total)
            for part in range(3):
                piece = level.astype(BF).astype(F32)
                stat = jnp.where(lane == 8 * part + head, piece, stat)
                level = level - piece
        else:
            sum_out_ref[0, :, left : left + HEAD] = summed
            stat = jnp.where(lane == head, row_max, stat)
            stat = jnp.where(lane == 8 + head, total, stat)
    if last:
        out_ref[0, :, query_ref.shape[2] :] = stat.astype(BF)
    else:
        stat_out_ref[0] = stat


def attend(query_segments, queries, chunks, state, last):
    groups, count, width = queries.shape
    keys = 2 * ROWS * len(chunks)
    first = state is None
    block = lambda *tail: pl.BlockSpec((1,) + tail, lambda i: (i,) + (0,) * len(tail))
    sum_shape = jax.ShapeDtypeStruct((groups, count, width), F32)
    stat_shape = jax.ShapeDtypeStruct((groups, count, HEAD), F32)
    out_shape = (
        jax.ShapeDtypeStruct((groups, count, width + HEAD), BF) if last else (sum_shape, stat_shape)
    )
    return pl.pallas_call(
        functools.partial(attend_kernel, first, last, len(chunks)),
        grid=(groups,),
        out_shape=out_shape,
        in_specs=[block(count, HEAD), block(count, width)]
        + [pl.BlockSpec((2, PACK, 2 * HEAD), lambda i: (0, 0, 0))] * len(chunks)
        + ([] if first else [block(count, width), block(count, HEAD)]),
        out_specs=block(count, width + HEAD) if last else (block(count, width), block(count, HEAD)),
        scratch_shapes=[
            pltpu.VMEM((keys, HEAD), BF),
            pltpu.VMEM((keys, 2 * HEAD), BF),
            pltpu.VMEM((8, keys), F32),
            pltpu.VMEM((count, keys), F32),
        ],
        compiler_params=pltpu.CompilerParams(vmem_limit_bytes=VMEM),
        cost_estimate=pl.CostEstimate(
            flops=8 * groups * count * width * keys,
            bytes_accessed=groups * count * width * 8,
            transcendentals=groups * count * 8 * keys,
        ),
        name="attend",
    )(query_segments, queries, *chunks, *(() if first else state))


def merge_kernel(own_ref, *refs):
    out_ref = refs[-1]
    width = out_ref.shape[2]
    sources = [own_ref] + list(refs[:-1])
    count = out_ref.shape[1]
    for half in range(2):
        rows = slice(half * count, (half + 1) * count)
        stats = [ref[0, rows, width:].astype(F32) for ref in sources]
        for head in range(width // HEAD):
            left = head * HEAD
            levels = [
                stat[:, head : head + 1] + stat[:, 8 + head : 9 + head] + stat[:, 16 + head : 17 + head]
                for stat in stats
            ]
            top = functools.reduce(jnp.maximum, levels)
            shares = [jnp.exp2(level - top) for level in levels]
            whole = functools.reduce(jnp.add, shares)
            out_ref[half, :, left : left + HEAD] = functools.reduce(
                jnp.add,
                [
                    share / whole * ref[0, rows, left : left + HEAD].astype(F32)
                    for share, ref in zip(shares, sources)
                ],
            ).astype(BF)


def merge(parts):
    _, count, width = parts[0].shape
    return pl.pallas_call(
        merge_kernel,
        out_shape=jax.ShapeDtypeStruct((2, count // 2, width - HEAD), BF),
        in_specs=[pl.BlockSpec(memory_space=pltpu.VMEM)] * len(parts),
        out_specs=pl.BlockSpec(memory_space=pltpu.VMEM),
        compiler_params=pltpu.CompilerParams(vmem_limit_bytes=VMEM),
        name="merge",
    )(*parts)


def rotation(positions):
    half = HEAD // 2
    inv_freq = jnp.exp(jnp.arange(half).astype(F32) * (-2.0 * math.log(1000000.0) / HEAD))
    angles = positions[:, None] * inv_freq[None, :]
    cosine, sine = jnp.cos(angles) * KEY_SCALE, jnp.sin(angles) * KEY_SCALE
    return jnp.concatenate([cosine, cosine], axis=1), jnp.concatenate([-sine, sine], axis=1)


def local(
    context,
    visual,
    visual_slots,
    norm_gain,
    key_value_weight,
    key_value_bias,
    queries,
    key_segments,
    query_segments,
):
    rank = lax.axis_index("ctx")
    core = lax.rem(rank, 2)
    first_row = rank * context.shape[0]
    where = jnp.stack([core, lax.axis_index("tp")]).astype(jnp.int32)

    visual_parts = gather_features(visual)

    up_to = jnp.sum(
        (key_segments[None, :] <= jnp.arange(HEAD, dtype=jnp.int32)[:, None]).astype(jnp.int32), axis=1
    )
    meta = gather_meta(jnp.stack([visual_slots, up_to, query_segments]))
    all_slots = meta[:, :, :, 0].reshape(32, HEAD)
    bounds = jnp.sum(meta[:, :, :, 1].reshape(32, HEAD), axis=0)[:16]

    def segments_of(positions):
        value = jnp.sum((bounds[:, None] <= positions[None, :]).astype(jnp.int32), axis=0)
        row = jnp.concatenate([value, jnp.zeros_like(value)]).astype(BF)
        return jnp.broadcast_to(row[None, :], (PACK - ROWS, 2 * HEAD))

    width = queries.shape[1] // 2
    mine = lax.dynamic_slice_in_dim(queries, core * width, width, 1)
    other = lax.dynamic_slice_in_dim(queries, (1 - core) * width, width, 1)
    mine = jnp.concatenate([mine, swap_cores(other)], axis=0)
    all_queries = jnp.stack([mine] + [shift_queries(mine, k) for k in SHIFTS[1:]])
    token_segments = jnp.where(core == 0, meta[:, :, 0, 2], meta[:, 0, :, 2])
    token_segments = jnp.transpose(token_segments, (1, 0, 2)).reshape(4, -1).astype(F32)
    token_segments = jnp.broadcast_to(token_segments[:, :, None], token_segments.shape + (HEAD,))

    kept, kept_positions = compact(
        context, all_slots, first_row, context.shape[0] - visual.shape[0]
    )
    kept_positions = kept_positions[:, 0]

    def key_values(parts, positions):
        cosine, sine = rotation(positions.astype(F32))
        mine, other = project(
            where,
            parts,
            norm_gain,
            key_value_weight,
            key_value_bias,
            cosine,
            sine,
            segments_of(positions.astype(jnp.int32)),
        )
        pair = jnp.stack([mine, swap_cores(other)])
        return [pair] + [shift_keys(pair, k) for k in SHIFTS[1:]]

    state = attend(token_segments, all_queries, key_values(visual_parts, visual_slots), None, False)
    for i in range(2):
        rows = slice(i * ROWS, (i + 1) * ROWS)
        chunk = key_values(gather_features(kept[rows]), kept_positions[rows])
        state = attend(token_segments, all_queries, chunk, state, i == 1)
    parts = [state[0:1]] + [
        shift_queries(state[i : i + 1], -SHIFTS[i]) for i in range(1, 4)
    ]
    merged = merge(parts)
    received = swap_cores(merged[1])
    kept_half = merged[0]
    return jnp.where(
        core == 0,
        jnp.concatenate([kept_half, received], axis=1),
        jnp.concatenate([received, kept_half], axis=1),
    )


def solution(mesh):
    in_specs = (
        P("ctx", "tp"),
        P("ctx", "tp"),
        P("ctx"),
        P(),
        P(None, "tp"),
        P("tp"),
        P("ctx", "tp"),
        P("ctx"),
        P("ctx"),
    )
    out_specs = P("ctx", "tp")
    return jax.shard_map(local, mesh=mesh, in_specs=in_specs, out_specs=out_specs, check_vma=False)
```

```python
import functools
import math

import jax
import jax.numpy as jnp
from jax import lax
from jax.experimental import pallas as pl
from jax.experimental.pallas import tpu as pltpu
from jax.sharding import PartitionSpec as P

HEAD = 128
BF = jnp.bfloat16
F32 = jnp.float32
NEG = -1e30
KEY_SCALE = HEAD**-0.5 * math.log2(math.e)
ROWS = 128
PACK = 144
SHIFTS = (0, 1, -1, 2)
BLOCK = 256
VMEM = 12 * 1024 * 1024


def index_of(x, y, core):
    return ((x % 4) * 4 + y % 4) * 2 + core


def devices_of_ctx():
    return [(x, y, core) for x in range(4) for y in range(4) for core in range(2)]


def swap_cores(value):
    perm = [(index_of(x, y, c), index_of(x, y, 1 - c)) for x, y, c in devices_of_ctx()]
    return lax.ppermute(value, "ctx", perm)


def shift_keys(value, by):
    perm = [
        (index_of(x, y, c), index_of(x + by, y, c) if c == 0 else index_of(x, y + by, c))
        for x, y, c in devices_of_ctx()
    ]
    return lax.ppermute(value, "ctx", perm)


def flip_queries(value, by):
    perm = [
        (index_of(x, y, c), index_of(x, y ^ by, c) if c == 0 else index_of(x ^ by, y, c))
        for x, y, c in devices_of_ctx()
    ]
    return lax.ppermute(value, "ctx", perm)


def flip_xy(value, by_x, by_y):
    perm = [(index_of(x, y, c), index_of(x ^ by_x, y ^ by_y, c)) for x, y, c in devices_of_ctx()]
    return lax.ppermute(value, "ctx", perm)


def shift_z(value, by):
    return lax.ppermute(value, "tp", [(i, (i + by) % 4) for i in range(4)])


def send_near(rows):
    return shift_z(rows, 1), shift_z(rows, -1)


def send_far(low, high):
    half = low.shape[0] // 2
    return shift_z(low[:half], 1), shift_z(high[half:], -1)


def after(value, *others):
    return lax.optimization_barrier((value, others))[0]


def gather_meta(meta):
    for by in (1, 2):
        meta = meta[None] if by == 1 else meta
        meta = jnp.concatenate([meta, flip_xy(meta, by, 0)])
    meta = meta[None]
    for by in (1, 2):
        meta = jnp.concatenate([meta, flip_xy(meta, 0, by)])
    return meta


def compact_kernel(first_ref, slots_ref, context_ref, rows_ref, positions_ref):
    total, kept = context_ref.shape[0], rows_ref.shape[0]
    place = lax.broadcasted_iota(jnp.int32, (total, HEAD), 0) + first_ref[0]
    hit = jnp.zeros((total, HEAD), F32)
    for i in range(slots_ref.shape[0]):
        hit = jnp.where(place == slots_ref[i : i + 1, :], 1.0, hit)
    hit = jnp.max(hit, axis=1, keepdims=True)
    keep = jnp.broadcast_to(1.0 - hit, (total, HEAD)).astype(BF)
    row = lax.broadcasted_iota(jnp.int32, (total, total), 0)
    col = lax.broadcasted_iota(jnp.int32, (total, total), 1)
    over_rows = (((0,), (0,)), ((), ()))
    before = lax.dot_general(
        keep, (row < col).astype(F32).astype(BF), over_rows, preferred_element_type=F32
    )
    itself = lax.dot_general(
        keep, (row == col).astype(F32).astype(BF), over_rows, preferred_element_type=F32
    )
    rank = jnp.where(itself > 0.5, before, -1.0)[0:1, :]
    want = lax.broadcasted_iota(jnp.int32, (kept, total), 0).astype(F32)
    pick = jnp.where(rank == want, 1.0, 0.0)
    source = lax.broadcasted_iota(jnp.int32, (kept, total), 1).astype(F32)
    positions_ref[...] = jnp.broadcast_to(
        jnp.sum(pick * source, axis=1, keepdims=True), (kept, HEAD)
    ) + first_ref[0].astype(F32)
    rows_ref[...] = jnp.dot(pick.astype(BF), context_ref[...], preferred_element_type=F32).astype(
        BF
    )


def compact(context, slots, first_row, kept):
    return pl.pallas_call(
        compact_kernel,
        out_shape=(
            jax.ShapeDtypeStruct((kept, context.shape[1]), BF),
            jax.ShapeDtypeStruct((kept, HEAD), F32),
        ),
        in_specs=[
            pl.BlockSpec(memory_space=pltpu.SMEM),
            pl.BlockSpec(memory_space=pltpu.VMEM),
            pl.BlockSpec(memory_space=pltpu.VMEM),
        ],
        out_specs=[pl.BlockSpec(memory_space=pltpu.VMEM)] * 2,
        compiler_params=pltpu.CompilerParams(vmem_limit_bytes=VMEM),
        name="compact",
    )(first_row.reshape(1), slots, context)


def hold_kernel(source_ref, held_ref, sem):
    copy = pltpu.make_async_copy(source_ref, held_ref, sem)
    copy.start()
    copy.wait()


def hold(value):
    return pl.pallas_call(
        hold_kernel,
        in_specs=[pl.BlockSpec(memory_space=pl.ANY)],
        out_specs=pl.BlockSpec(memory_space=pltpu.VMEM),
        out_shape=pltpu.VMEM(value.shape, value.dtype),
        scratch_shapes=[pltpu.SemaphoreType.DMA],
        compiler_params=pltpu.CompilerParams(vmem_limit_bytes=VMEM),
        cost_estimate=pl.CostEstimate(
            flops=0, bytes_accessed=3 * value.size, transcendentals=0
        ),
        name="hold",
    )(value)


def project_kernel(
    where_ref,
    own_ref,
    low_ref,
    high_ref,
    far_low_ref,
    far_high_ref,
    gain_ref,
    weight_ref,
    bias_ref,
    cosine_ref,
    sine_ref,
    segment_ref,
    mine_ref,
    other_ref,
):
    features = own_ref.shape[1]
    order = [lax.rem(where_ref[1] + away, 4) for away in (0, 3, 1, 2)]
    parts = [
        own_ref[...],
        low_ref[...],
        high_ref[...],
        jnp.concatenate([far_low_ref[...], far_high_ref[...]], axis=0),
    ]
    squares = jnp.zeros((ROWS, 1), F32)
    total = None
    for i, part in enumerate(parts):
        wide = part.astype(F32)
        squares = squares + jnp.sum(wide * wide, axis=1, keepdims=True)
        gained = (wide * gain_ref[order[i]]).astype(BF)
        start = pl.multiple_of(order[i] * features, features)
        term = jnp.dot(gained, weight_ref[pl.ds(start, features), :], preferred_element_type=F32)
        total = term if total is None else total + term
    total = total * lax.rsqrt(squares / (4 * features) + 1e-06) + bias_ref[...].astype(F32)
    cosine, sine = cosine_ref[...], sine_ref[...]
    packed = []
    for head in range(2):
        left = head * 2 * HEAD
        key = total[:, left : left + HEAD]
        key = key * cosine + pltpu.roll(key, HEAD // 2, 1) * sine
        packed.append(
            jnp.concatenate([key, total[:, left + HEAD : left + 2 * HEAD]], axis=1).astype(BF)
        )
    mine = where_ref[0] == 0
    mine_ref[0:ROWS, :] = jnp.where(mine, packed[0], packed[1])
    other_ref[0:ROWS, :] = jnp.where(mine, packed[1], packed[0])
    mine_ref[ROWS:PACK, :] = segment_ref[...]
    other_ref[ROWS:PACK, :] = segment_ref[...]


def project(where, parts, gain, weight, bias, cosine, sine, segment):
    features, columns = parts[0].shape[1], weight.shape[1]
    vmem = pl.BlockSpec(memory_space=pltpu.VMEM)
    return pl.pallas_call(
        project_kernel,
        in_specs=[pl.BlockSpec(memory_space=pltpu.SMEM)]
        + [vmem] * 11,
        out_specs=[vmem] * 2,
        out_shape=(jax.ShapeDtypeStruct((PACK, 2 * HEAD), BF),) * 2,
        compiler_params=pltpu.CompilerParams(vmem_limit_bytes=VMEM),
        cost_estimate=pl.CostEstimate(
            flops=4 * ROWS * 4 * features * columns,
            bytes_accessed=2 * 4 * features * (columns + ROWS),
            transcendentals=0,
        ),
        name="project",
    )(where, *parts, gain, weight, bias.reshape(1, columns), cosine, sine, segment)


def attend_kernel(first, last, blocks, *refs):
    query_segments_ref, query_ref = refs[:2]
    key_refs = refs[2 : 2 + blocks]
    refs = refs[2 + blocks :]
    if not first:
        sum_in_ref, stat_in_ref = refs[:2]
        refs = refs[2:]
    if last:
        out_ref = refs[0]
        refs = refs[1:]
    else:
        sum_out_ref, stat_out_ref = refs[:2]
        refs = refs[2:]
    key_ref, value_ref, segment_ref, bias_ref = refs
    keys = key_ref.shape[0]

    for i, ref in enumerate(key_refs):
        for j in range(2):
            start = (2 * i + j) * ROWS
            key_ref[start : start + ROWS, :] = ref[j, 0:ROWS, 0:HEAD]
            value_ref[start : start + ROWS, 0:HEAD] = ref[j, 0:ROWS, HEAD:]
            segment_ref[:, start : start + ROWS] = jnp.broadcast_to(
                ref[j, ROWS:PACK, 0:ROWS].astype(F32)[0:1, :], (8, ROWS)
            )
    value_ref[:, HEAD:] = jnp.ones((keys, HEAD), BF)

    count, width = query_ref.shape
    query_segments = query_segments_ref[...]
    bias_ref[...] = jnp.where(segment_ref[0:1, :] <= query_segments[:, 0:1], 0.0, NEG)
    lane = lax.broadcasted_iota(jnp.int32, (count, HEAD), 1)
    stat = jnp.zeros((count, HEAD), F32)
    for head in range(width // HEAD):
        left = head * HEAD
        scores = [
            lax.dot_general(
                query_ref[:, left : left + HEAD],
                key_ref[at : at + BLOCK, :],
                (((1,), (1,)), ((), ())),
                preferred_element_type=F32,
            )
            + bias_ref[:, at : at + BLOCK]
            for at in range(0, keys, BLOCK)
        ]
        tops = [jnp.max(score, axis=1, keepdims=True) for score in scores]
        if not first:
            before = jnp.max(
                jnp.where(lane == head, stat_in_ref[...], -jnp.inf), axis=1, keepdims=True
            )
            tops.append(before)
        row_max = functools.reduce(jnp.maximum, tops)
        summed = functools.reduce(
            jnp.add,
            [
                jnp.dot(
                    jnp.exp2(score - row_max).astype(BF),
                    value_ref[i * BLOCK : (i + 1) * BLOCK, :],
                    preferred_element_type=F32,
                )
                for i, score in enumerate(scores)
            ],
        )
        stat = jnp.where(lane == head, row_max, stat)
        stat = jnp.where(lane == 8 + head, summed[:, HEAD:], stat)
        summed = summed[:, 0:HEAD]
        if not first:
            summed = summed + jnp.exp2(before - row_max) * sum_in_ref[:, left : left + HEAD]
        if last:
            out_ref[:, left : left + HEAD] = summed.astype(BF)
        else:
            sum_out_ref[:, left : left + HEAD] = summed
    if not first:
        stat_in = stat_in_ref[...]
        factor = pltpu.roll(jnp.exp2(stat_in - stat), 8, 1)
        stat = stat + jnp.where((lane >= 8) & (lane < 16), factor * stat_in, 0.0)
    if last:
        high = stat.astype(BF).astype(F32)
        middle = (stat - high).astype(BF).astype(F32)
        low = stat - high - middle
        coded = jnp.where(
            lane < 16,
            high,
            jnp.where(lane < 32, pltpu.roll(middle, 16, 1), pltpu.roll(low, 32, 1)),
        )
        out_ref[:, width:] = coded.astype(BF)
    else:
        stat_out_ref[...] = stat


def attend(query_segments, queries, chunks, state, last):
    count, width = queries.shape
    keys = 2 * ROWS * len(chunks)
    first = state is None
    vmem = pl.BlockSpec(memory_space=pltpu.VMEM)
    sum_shape = jax.ShapeDtypeStruct((count, width), F32)
    stat_shape = jax.ShapeDtypeStruct((count, HEAD), F32)
    out_shape = (
        jax.ShapeDtypeStruct((count, width + HEAD), BF) if last else (sum_shape, stat_shape)
    )
    operands = (query_segments, queries, *chunks, *(() if first else state))
    return pl.pallas_call(
        functools.partial(attend_kernel, first, last, len(chunks)),
        out_shape=out_shape,
        in_specs=[vmem] * len(operands),
        out_specs=vmem if last else (vmem, vmem),
        scratch_shapes=[
            pltpu.VMEM((keys, HEAD), BF),
            pltpu.VMEM((keys, 2 * HEAD), BF),
            pltpu.VMEM((8, keys), F32),
            pltpu.VMEM((count, keys), F32),
        ],
        compiler_params=pltpu.CompilerParams(vmem_limit_bytes=VMEM),
        cost_estimate=pl.CostEstimate(
            flops=18 * count * width * keys,
            bytes_accessed=count * width * 8,
            transcendentals=count * 8 * keys,
        ),
        name="attend",
    )(*operands)


def merge_kernel(start, *refs):
    sources, out_ref = refs[:-1], refs[-1]
    count, width = out_ref.shape
    rows = slice(start, start + count)
    stats = []
    for ref in sources:
        coded = ref[rows, width:].astype(F32)
        stats.append(coded + pltpu.roll(coded, HEAD - 16, 1) + pltpu.roll(coded, HEAD - 32, 1))
    top = functools.reduce(jnp.maximum, stats)
    shares = [jnp.exp2(stat - top) for stat in stats]
    whole = functools.reduce(
        jnp.add, [share * pltpu.roll(stat, HEAD - 8, 1) for share, stat in zip(shares, stats)]
    )
    shares = [share / whole for share in shares]
    for head in range(width // HEAD):
        left = head * HEAD
        out_ref[:, left : left + HEAD] = functools.reduce(
            jnp.add,
            [
                share[:, head : head + 1] * ref[rows, left : left + HEAD].astype(F32)
                for share, ref in zip(shares, sources)
            ],
        ).astype(BF)


def merge(parts, half):
    count, width = parts[0].shape
    vmem = pl.BlockSpec(memory_space=pltpu.VMEM)
    return pl.pallas_call(
        functools.partial(merge_kernel, half * count // 2),
        out_shape=jax.ShapeDtypeStruct((count // 2, width - HEAD), BF),
        in_specs=[vmem] * len(parts),
        out_specs=vmem,
        compiler_params=pltpu.CompilerParams(vmem_limit_bytes=VMEM),
        name="merge",
    )(*parts)


def rotation(positions):
    half = HEAD // 2
    inv_freq = jnp.exp(jnp.arange(half).astype(F32) * (-2.0 * math.log(1000000.0) / HEAD))
    angles = positions[:, None] * inv_freq[None, :]
    cosine, sine = jnp.cos(angles) * KEY_SCALE, jnp.sin(angles) * KEY_SCALE
    return jnp.concatenate([cosine, cosine], axis=1), jnp.concatenate([-sine, sine], axis=1)


def local(
    context,
    visual,
    visual_slots,
    norm_gain,
    key_value_weight,
    key_value_bias,
    queries,
    key_segments,
    query_segments,
):
    rank = lax.axis_index("ctx")
    core = lax.rem(rank, 2)
    first_row = rank * context.shape[0]
    where = jnp.stack([core, lax.axis_index("tp")]).astype(jnp.int32)

    visual_near = send_near(visual)

    width = queries.shape[1] // 2
    mine = lax.dynamic_slice_in_dim(queries, core * width, width, 1)
    other = lax.dynamic_slice_in_dim(queries, (1 - core) * width, width, 1)
    mine = jnp.concatenate([mine, swap_cores(other)], axis=0)
    near = flip_queries(mine, 1)
    far = flip_queries(jnp.concatenate([mine, near], axis=0), 3)
    tokens = mine.shape[0]
    all_queries = [mine, near, far[tokens:], far[:tokens]]
    up_to = jnp.sum(
        (key_segments[None, :] <= jnp.arange(HEAD, dtype=jnp.int32)[:, None]).astype(jnp.int32), axis=1
    )
    meta = gather_meta(jnp.stack([visual_slots, up_to, query_segments]))
    visual_far = send_far(*visual_near)
    weight = hold(key_value_weight)
    meta = after(meta, *visual_near, near)
    meta = jnp.stack([meta, swap_cores(meta)])
    all_slots = meta[:, :, :, 0].reshape(32, HEAD)
    bounds = jnp.sum(meta[:, :, :, 1].reshape(32, HEAD), axis=0)[:16]

    def segments_of(positions):
        value = jnp.sum((bounds[:, None] <= positions[None, :]).astype(jnp.int32), axis=0)
        row = jnp.concatenate([value, jnp.zeros_like(value)]).astype(BF)
        return jnp.broadcast_to(row[None, :], (PACK - ROWS, 2 * HEAD))

    token_segments = jnp.where(core == 0, meta[:, :, 0, 2], meta[:, 0, :, 2])
    token_segments = jnp.transpose(token_segments, (1, 0, 2)).reshape(4, -1).astype(F32)
    token_segments = jnp.broadcast_to(token_segments[:, :, None], token_segments.shape + (HEAD,))

    all_slots = after(all_slots, weight)
    kept, kept_positions = compact(
        context, all_slots, first_row, context.shape[0] - visual.shape[0]
    )
    kept_positions = kept_positions[:, 0]
    gain = norm_gain.astype(F32).reshape(4, 1, -1)

    def pair_of(parts, positions):
        cosine, sine = rotation(positions.astype(F32))
        mine, other = project(
            where,
            parts,
            gain,
            weight,
            key_value_bias,
            cosine,
            sine,
            segments_of(positions.astype(jnp.int32)),
        )
        return jnp.stack([mine, swap_cores(other)])

    def spread(pair):
        return (pair, *(shift_keys(pair, k) for k in SHIFTS[1:]))

    kept_near = send_near(kept)

    visual_parts = (after(visual, kept), *visual_near, *visual_far)
    chunk = spread(after(pair_of(visual_parts, visual_slots), far))
    kept_near = after(kept_near, chunk)
    kept_parts = []
    for at in range(0, kept.shape[0], ROWS):
        rows, low, high = (value[at : at + ROWS] for value in (kept, *kept_near))
        kept_parts.append((rows, low, high, *send_far(low, high)))
    states = [attend(token_segments[i], all_queries[i], chunk, None, False) for i in range(4)]

    first_pair = pair_of(after(kept_parts[0], states[0][1], states[1][1]), kept_positions[:ROWS])
    first_chunk = spread(first_pair)
    second_pair = pair_of(kept_parts[1], kept_positions[ROWS:])
    first_chunk = after(first_chunk, second_pair)
    second_chunk = spread(second_pair)
    for i in range(4):
        states[i] = attend(token_segments[i], all_queries[i], first_chunk, states[i], False)
        if i == 1:
            first_chunk = after(first_chunk, second_chunk)
    parts = [None] * 4
    for i in (2, 3, 1, 0):
        part = attend(token_segments[i], all_queries[i], second_chunk, states[i], True)
        parts[i] = flip_queries(part, i) if i else part
    received = swap_cores(merge(parts, 1))
    kept_half = merge(parts, 0)
    return jnp.where(
        core == 0,
        jnp.concatenate([kept_half, received], axis=1),
        jnp.concatenate([received, kept_half], axis=1),
    )


def solution(mesh):
    in_specs = (
        P("ctx", "tp"),
        P("ctx", "tp"),
        P("ctx"),
        P(),
        P(None, "tp"),
        P("tp"),
        P("ctx", "tp"),
        P("ctx"),
        P("ctx"),
    )
    out_specs = P("ctx", "tp")
    return jax.shard_map(local, mesh=mesh, in_specs=in_specs, out_specs=out_specs, check_vma=False)
```

```python
import functools
import math

import jax
import jax.numpy as jnp
from jax import lax
from jax.experimental import pallas as pl
from jax.experimental.pallas import tpu as pltpu
from jax.sharding import PartitionSpec as P

HEAD = 128
BF = jnp.bfloat16
F32 = jnp.float32
NEG = -1e30
KEY_SCALE = HEAD**-0.5 * math.log2(math.e)
ROWS = 128
PACK = 144
BLOCK = 256
VMEM = 16 * 1024 * 1024


def index_of(x, y, core):
    return ((x % 4) * 4 + y % 4) * 2 + core


def devices_of_ctx():
    return [(x, y, core) for x in range(4) for y in range(4) for core in range(2)]


def swap_cores(value):
    perm = [(index_of(x, y, c), index_of(x, y, 1 - c)) for x, y, c in devices_of_ctx()]
    return lax.ppermute(value, "ctx", perm)


def shift_keys(value, by):
    perm = [
        (index_of(x, y, c), index_of(x + by, y, c) if c == 0 else index_of(x, y + by, c))
        for x, y, c in devices_of_ctx()
    ]
    return lax.ppermute(value, "ctx", perm)


def flip_queries(value, by):
    perm = [
        (index_of(x, y, c), index_of(x, y ^ by, c) if c == 0 else index_of(x ^ by, y, c))
        for x, y, c in devices_of_ctx()
    ]
    return lax.ppermute(value, "ctx", perm)


def flip_xy(value, by_x, by_y):
    perm = [(index_of(x, y, c), index_of(x ^ by_x, y ^ by_y, c)) for x, y, c in devices_of_ctx()]
    return lax.ppermute(value, "ctx", perm)


def shift_z(value, by):
    return lax.ppermute(value, "tp", [(i, (i + by) % 4) for i in range(4)])


def send_near(rows):
    return shift_z(rows, 1), shift_z(rows, -1)


def send_far(low, high):
    half = low.shape[0] // 2
    return shift_z(low[:half], 1), shift_z(high[half:], -1)


def after(value, *others):
    return lax.optimization_barrier((value, others))[0]


def gather_meta(meta):
    for by in (1, 2):
        meta = meta[None] if by == 1 else meta
        meta = jnp.concatenate([meta, flip_xy(meta, by, 0)])
    meta = meta[None]
    for by in (1, 2):
        meta = jnp.concatenate([meta, flip_xy(meta, 0, by)])
    return meta


def compact_kernel(first_ref, slots_ref, context_ref, rows_ref, positions_ref):
    total, kept = context_ref.shape[0], rows_ref.shape[0]
    place = lax.broadcasted_iota(jnp.int32, (total, HEAD), 0) + first_ref[0]
    hit = jnp.zeros((total, HEAD), F32)
    for i in range(slots_ref.shape[0]):
        hit = jnp.where(place == slots_ref[i : i + 1, :], 1.0, hit)
    hit = jnp.max(hit, axis=1, keepdims=True)
    keep = jnp.broadcast_to(1.0 - hit, (total, HEAD)).astype(BF)
    row = lax.broadcasted_iota(jnp.int32, (total, total), 0)
    col = lax.broadcasted_iota(jnp.int32, (total, total), 1)
    over_rows = (((0,), (0,)), ((), ()))
    before = lax.dot_general(
        keep, (row < col).astype(F32).astype(BF), over_rows, preferred_element_type=F32
    )
    itself = lax.dot_general(
        keep, (row == col).astype(F32).astype(BF), over_rows, preferred_element_type=F32
    )
    rank = jnp.where(itself > 0.5, before, -1.0)[0:1, :]
    want = lax.broadcasted_iota(jnp.int32, (kept, total), 0).astype(F32)
    pick = jnp.where(rank == want, 1.0, 0.0)
    source = lax.broadcasted_iota(jnp.int32, (kept, total), 1).astype(F32)
    positions_ref[...] = jnp.broadcast_to(
        jnp.sum(pick * source, axis=1, keepdims=True), (kept, HEAD)
    ) + first_ref[0].astype(F32)
    rows_ref[...] = jnp.dot(pick.astype(BF), context_ref[...], preferred_element_type=F32).astype(
        BF
    )


def compact(context, slots, first_row, kept):
    return pl.pallas_call(
        compact_kernel,
        out_shape=(
            jax.ShapeDtypeStruct((kept, context.shape[1]), BF),
            jax.ShapeDtypeStruct((kept, HEAD), F32),
        ),
        in_specs=[
            pl.BlockSpec(memory_space=pltpu.SMEM),
            pl.BlockSpec(memory_space=pltpu.VMEM),
            pl.BlockSpec(memory_space=pltpu.VMEM),
        ],
        out_specs=[pl.BlockSpec(memory_space=pltpu.VMEM)] * 2,
        compiler_params=pltpu.CompilerParams(vmem_limit_bytes=VMEM),
        name="compact",
    )(first_row.reshape(1), slots, context)


def hold_kernel(source_ref, held_ref, sem):
    copy = pltpu.make_async_copy(source_ref, held_ref, sem)
    copy.start()
    copy.wait()


def hold(value):
    return pl.pallas_call(
        hold_kernel,
        in_specs=[pl.BlockSpec(memory_space=pl.ANY)],
        out_specs=pl.BlockSpec(memory_space=pltpu.VMEM),
        out_shape=pltpu.VMEM(value.shape, value.dtype),
        scratch_shapes=[pltpu.SemaphoreType.DMA],
        compiler_params=pltpu.CompilerParams(vmem_limit_bytes=VMEM),
        cost_estimate=pl.CostEstimate(
            flops=0, bytes_accessed=3 * value.size, transcendentals=0
        ),
        name="hold",
    )(value)


def project_kernel(
    where_ref,
    own_ref,
    low_ref,
    high_ref,
    far_low_ref,
    far_high_ref,
    gain_ref,
    weight_ref,
    bias_ref,
    cosine_ref,
    sine_ref,
    segment_ref,
    mine_ref,
    other_ref,
):
    features = own_ref.shape[1]
    order = [lax.rem(where_ref[1] + away, 4) for away in (0, 3, 1, 2)]
    parts = [
        own_ref[...],
        low_ref[...],
        high_ref[...],
        jnp.concatenate([far_low_ref[...], far_high_ref[...]], axis=0),
    ]
    count = own_ref.shape[0]
    squares = jnp.zeros((count, 1), F32)
    total = None
    for i, part in enumerate(parts):
        wide = part.astype(F32)
        squares = squares + jnp.sum(wide * wide, axis=1, keepdims=True)
        gained = (wide * gain_ref[order[i]]).astype(BF)
        start = pl.multiple_of(order[i] * features, features)
        term = jnp.dot(gained, weight_ref[pl.ds(start, features), :], preferred_element_type=F32)
        total = term if total is None else total + term
    total = total * lax.rsqrt(squares / (4 * features) + 1e-06) + bias_ref[...].astype(F32)
    cosine, sine = cosine_ref[...], sine_ref[...]
    packed = []
    for head in range(2):
        left = head * 2 * HEAD
        key = total[:, left : left + HEAD]
        key = key * cosine + pltpu.roll(key, HEAD // 2, 1) * sine
        packed.append(
            jnp.concatenate([key, total[:, left + HEAD : left + 2 * HEAD]], axis=1).astype(BF)
        )
    mine = where_ref[0] == 0
    mine_rows = jnp.where(mine, packed[0], packed[1])
    other_rows = jnp.where(mine, packed[1], packed[0])
    for i in range(count // ROWS):
        for ref, rows in ((mine_ref, mine_rows), (other_ref, other_rows)):
            ref[i, 0:ROWS, :] = rows[i * ROWS : (i + 1) * ROWS, :]
            ref[i, ROWS:PACK, :] = segment_ref[i]


def project(where, parts, gain, weight, bias, cosine, sine, segment):
    (rows, features), columns = parts[0].shape, weight.shape[1]
    vmem = pl.BlockSpec(memory_space=pltpu.VMEM)
    return pl.pallas_call(
        project_kernel,
        in_specs=[pl.BlockSpec(memory_space=pltpu.SMEM)]
        + [vmem] * 11,
        out_specs=[vmem] * 2,
        out_shape=(jax.ShapeDtypeStruct((rows // ROWS, PACK, 2 * HEAD), BF),) * 2,
        compiler_params=pltpu.CompilerParams(vmem_limit_bytes=VMEM),
        cost_estimate=pl.CostEstimate(
            flops=4 * rows * 4 * features * columns,
            bytes_accessed=2 * 4 * features * (columns + rows),
            transcendentals=0,
        ),
        name="project",
    )(where, *parts, gain, weight, bias.reshape(1, columns), cosine, sine, segment)


def attend_kernel(first, last, blocks, *refs):
    query_segments_ref, query_ref = refs[:2]
    key_refs = refs[2 : 2 + blocks]
    refs = refs[2 + blocks :]
    if not first:
        sum_in_ref, stat_in_ref = refs[:2]
        refs = refs[2:]
    if last:
        out_ref = refs[0]
        refs = refs[1:]
    else:
        sum_out_ref, stat_out_ref = refs[:2]
        refs = refs[2:]
    key_ref, value_ref, segment_ref, bias_ref = refs
    keys = key_ref.shape[0]

    start = 0
    for ref in key_refs:
        for j in range(ref.shape[0]):
            key_ref[start : start + ROWS, :] = ref[j, 0:ROWS, 0:HEAD]
            value_ref[start : start + ROWS, 0:HEAD] = ref[j, 0:ROWS, HEAD:]
            segment_ref[:, start : start + ROWS] = jnp.broadcast_to(
                ref[j, ROWS:PACK, 0:ROWS].astype(F32)[0:1, :], (8, ROWS)
            )
            start += ROWS
    value_ref[:, HEAD:] = jnp.ones((keys, HEAD), BF)

    count, width = query_ref.shape
    query_segments = query_segments_ref[...]
    bias_ref[...] = jnp.where(segment_ref[0:1, :] <= query_segments[:, 0:1], 0.0, NEG)
    lane = lax.broadcasted_iota(jnp.int32, (count, HEAD), 1)
    stat = jnp.zeros((count, HEAD), F32)
    for head in range(width // HEAD):
        left = head * HEAD
        scores = [
            lax.dot_general(
                query_ref[:, left : left + HEAD],
                key_ref[at : at + BLOCK, :],
                (((1,), (1,)), ((), ())),
                preferred_element_type=F32,
            )
            + bias_ref[:, at : at + BLOCK]
            for at in range(0, keys, BLOCK)
        ]
        tops = [jnp.max(score, axis=1, keepdims=True) for score in scores]
        if not first:
            before = jnp.max(
                jnp.where(lane == head, stat_in_ref[...], -jnp.inf), axis=1, keepdims=True
            )
            tops.append(before)
        row_max = functools.reduce(jnp.maximum, tops)
        summed = functools.reduce(
            jnp.add,
            [
                jnp.dot(
                    jnp.exp2(score - row_max).astype(BF),
                    value_ref[i * BLOCK : (i + 1) * BLOCK, :],
                    preferred_element_type=F32,
                )
                for i, score in enumerate(scores)
            ],
        )
        stat = jnp.where(lane == head, row_max, stat)
        stat = jnp.where(lane == 8 + head, summed[:, HEAD:], stat)
        summed = summed[:, 0:HEAD]
        if not first:
            summed = summed + jnp.exp2(before - row_max) * sum_in_ref[:, left : left + HEAD]
        if last:
            out_ref[:, left : left + HEAD] = summed.astype(BF)
        else:
            sum_out_ref[:, left : left + HEAD] = summed
    if not first:
        stat_in = stat_in_ref[...]
        factor = pltpu.roll(jnp.exp2(stat_in - stat), 8, 1)
        stat = stat + jnp.where((lane >= 8) & (lane < 16), factor * stat_in, 0.0)
    if last:
        high = stat.astype(BF).astype(F32)
        middle = (stat - high).astype(BF).astype(F32)
        low = stat - high - middle
        coded = jnp.where(
            lane < 16,
            high,
            jnp.where(lane < 32, pltpu.roll(middle, 16, 1), pltpu.roll(low, 32, 1)),
        )
        out_ref[:, width:] = coded.astype(BF)
    else:
        stat_out_ref[...] = stat


def attend(query_segments, queries, chunks, state, last):
    count, width = queries.shape
    keys = ROWS * sum(chunk.shape[0] for chunk in chunks)
    first = state is None
    vmem = pl.BlockSpec(memory_space=pltpu.VMEM)
    sum_shape = jax.ShapeDtypeStruct((count, width), F32)
    stat_shape = jax.ShapeDtypeStruct((count, HEAD), F32)
    out_shape = (
        jax.ShapeDtypeStruct((count, width + HEAD), BF) if last else (sum_shape, stat_shape)
    )
    operands = (query_segments, queries, *chunks, *(() if first else state))
    return pl.pallas_call(
        functools.partial(attend_kernel, first, last, len(chunks)),
        out_shape=out_shape,
        in_specs=[vmem] * len(operands),
        out_specs=vmem if last else (vmem, vmem),
        scratch_shapes=[
            pltpu.VMEM((keys, HEAD), BF),
            pltpu.VMEM((keys, 2 * HEAD), BF),
            pltpu.VMEM((8, keys), F32),
            pltpu.VMEM((count, keys), F32),
        ],
        compiler_params=pltpu.CompilerParams(vmem_limit_bytes=VMEM),
        cost_estimate=pl.CostEstimate(
            flops=18 * count * width * keys,
            bytes_accessed=count * width * 8,
            transcendentals=count * 8 * keys,
        ),
        name="attend",
    )(*operands)


def merge_kernel(start, *refs):
    sources, out_ref = refs[:-1], refs[-1]
    count, width = out_ref.shape
    rows = slice(start, start + count)
    stats = []
    for ref in sources:
        coded = ref[rows, width:].astype(F32)
        stats.append(coded + pltpu.roll(coded, HEAD - 16, 1) + pltpu.roll(coded, HEAD - 32, 1))
    top = functools.reduce(jnp.maximum, stats)
    shares = [jnp.exp2(stat - top) for stat in stats]
    whole = functools.reduce(
        jnp.add, [share * pltpu.roll(stat, HEAD - 8, 1) for share, stat in zip(shares, stats)]
    )
    shares = [share / whole for share in shares]
    for head in range(width // HEAD):
        left = head * HEAD
        out_ref[:, left : left + HEAD] = functools.reduce(
            jnp.add,
            [
                share[:, head : head + 1] * ref[rows, left : left + HEAD].astype(F32)
                for share, ref in zip(shares, sources)
            ],
        ).astype(BF)


def merge(parts, half):
    count, width = parts[0].shape
    vmem = pl.BlockSpec(memory_space=pltpu.VMEM)
    return pl.pallas_call(
        functools.partial(merge_kernel, half * count // 2),
        out_shape=jax.ShapeDtypeStruct((count // 2, width - HEAD), BF),
        in_specs=[vmem] * len(parts),
        out_specs=vmem,
        compiler_params=pltpu.CompilerParams(vmem_limit_bytes=VMEM),
        name="merge",
    )(*parts)


def rotation(positions):
    half = HEAD // 2
    inv_freq = jnp.exp(jnp.arange(half).astype(F32) * (-2.0 * math.log(1000000.0) / HEAD))
    angles = positions[:, None] * inv_freq[None, :]
    cosine, sine = jnp.cos(angles) * KEY_SCALE, jnp.sin(angles) * KEY_SCALE
    return jnp.concatenate([cosine, cosine], axis=1), jnp.concatenate([-sine, sine], axis=1)


def local(
    context,
    visual,
    visual_slots,
    norm_gain,
    key_value_weight,
    key_value_bias,
    queries,
    key_segments,
    query_segments,
):
    rank = lax.axis_index("ctx")
    core = lax.rem(rank, 2)
    first_row = rank * context.shape[0]
    where = jnp.stack([core, lax.axis_index("tp")]).astype(jnp.int32)

    visual_near = send_near(visual)

    width = queries.shape[1] // 2
    mine = lax.dynamic_slice_in_dim(queries, core * width, width, 1)
    other = lax.dynamic_slice_in_dim(queries, (1 - core) * width, width, 1)
    mine = jnp.concatenate([mine, swap_cores(other)], axis=0)
    near = flip_queries(mine, 1)
    far = flip_queries(jnp.concatenate([mine, near], axis=0), 3)
    tokens = mine.shape[0]
    all_queries = [mine, near, far[tokens:], far[:tokens]]
    up_to = jnp.sum(
        (key_segments[None, :] <= jnp.arange(HEAD, dtype=jnp.int32)[:, None]).astype(jnp.int32), axis=1
    )
    meta = gather_meta(jnp.stack([visual_slots, up_to, query_segments]))
    visual_far = send_far(*visual_near)
    weight = hold(key_value_weight)
    meta = after(meta, *visual_near, near)
    meta = jnp.stack([meta, swap_cores(meta)])
    all_slots = meta[:, :, :, 0].reshape(32, HEAD)
    bounds = jnp.sum(meta[:, :, :, 1].reshape(32, HEAD), axis=0)[:16]

    def segments_of(positions):
        value = jnp.sum((bounds[:, None] <= positions[None, :]).astype(jnp.int32), axis=0)
        value = value.astype(BF).reshape(-1, 1, ROWS)
        row = jnp.concatenate([value, jnp.zeros_like(value)], axis=2)
        return jnp.broadcast_to(row, (row.shape[0], PACK - ROWS, 2 * HEAD))

    token_segments = jnp.where(core == 0, meta[:, :, 0, 2], meta[:, 0, :, 2])
    token_segments = jnp.transpose(token_segments, (1, 0, 2)).reshape(4, -1).astype(F32)
    token_segments = jnp.broadcast_to(token_segments[:, :, None], token_segments.shape + (HEAD,))

    all_slots = after(all_slots, weight)
    kept, kept_positions = compact(
        context, all_slots, first_row, context.shape[0] - visual.shape[0]
    )
    kept_positions = kept_positions[:, 0]
    gain = norm_gain.astype(F32).reshape(4, 1, -1)

    def pair_of(parts, positions):
        cosine, sine = rotation(positions.astype(F32))
        mine, other = project(
            where,
            parts,
            gain,
            weight,
            key_value_bias,
            cosine,
            sine,
            segments_of(positions.astype(jnp.int32)),
        )
        return jnp.concatenate([mine, swap_cores(other)])

    def spread(pair, *before_last):
        return (
            pair,
            shift_keys(pair, 1),
            shift_keys(pair, -1),
            shift_keys(after(pair, *before_last), 2),
        )

    kept_near = send_near(kept)

    visual_parts = (after(visual, kept), *visual_near, *visual_far)
    chunk = spread(pair_of(visual_parts, visual_slots), far)
    states = [attend(token_segments[i], all_queries[i], chunk, None, False) for i in range(4)]
    kept_near = after(kept_near, states[0][1], states[1][1])
    kept_parts = (kept, *kept_near, *send_far(*kept_near))
    chunk = spread(pair_of(after(kept_parts, states[2][1]), kept_positions))
    parts = [None] * 4
    for i in (2, 3, 1, 0):
        part = attend(token_segments[i], all_queries[i], chunk, states[i], True)
        parts[i] = flip_queries(part, i) if i else part
    received = swap_cores(merge(parts, 1))
    kept_half = merge(parts, 0)
    return jnp.where(
        core == 0,
        jnp.concatenate([kept_half, received], axis=1),
        jnp.concatenate([received, kept_half], axis=1),
    )


def solution(mesh):
    in_specs = (
        P("ctx", "tp"),
        P("ctx", "tp"),
        P("ctx"),
        P(),
        P(None, "tp"),
        P("tp"),
        P("ctx", "tp"),
        P("ctx"),
        P("ctx"),
    )
    out_specs = P("ctx", "tp")
    return jax.shard_map(local, mesh=mesh, in_specs=in_specs, out_specs=out_specs, check_vma=False)
```
